32 devices in a mesh: az: 4 (over y, x), col: 8 (over z, core).
Axes of the slice: x: 2, y: 2, z: 4, core: 2. Of those that a mesh axis runs over, the one named last changes fastest.
Arguments:
- phase_field: float32 [64, 1024, 2048], P(None, 'col', 'az'), may hold values from -1 to 1
- velocity: bfloat16 [2, 64, 1024, 2048], P(None, None, 'col', 'az'), may hold values from -4 to 4
- owned_modes: int32 [32, 16], replicated, may hold values from 0 to 511, as said below
- legendre: bfloat16 [512, 1024, 512], P(('az', 'col')), as said below
- radial_inverse: bfloat16 [512, 64, 64], replicated, as said below
Outputs:
- new_phase: float32 [64, 1024, 2048], P(None, 'col', 'az')
The draws below stay inside these ranges and needn't reach their ends.
Inputs may be any that keep to these rules, and one draw needn't show every extreme that they name: `owned_modes`: every order from 0 to 511 appears exactly once; the second half of each row is 511 minus its first half. legendre[q, t, l] is the orthonormal associated Legendre function of degree l and order m_q (owned_modes flattened at q) at cos(theta_t), normalized so that the integral of its square times sin(theta) over theta is 1, rounded to bfloat16; it is 0 for l < m_q. `radial_inverse`: one matrix for each degree.
All inputs are finite; a program needn't handle non-finite values.
Results may differ from the reference program's by a relative error of at most 0.0003.
Values sent between devices are 32-bit elements; how exact they have to be, the bound alone decides.
A program may use at most 256 MiB of HBM per device.

```python
import math
import jax
import jax.numpy as jnp
from jax import lax

NP = 2048
NT = 1024
DEGREES = 512
SHELLS = 64
MODES_DEV = 16


def ownership(key):
    pair_key = jax.random.fold_in(key, 23)
    pair_count = DEGREES // 2
    pair_order = jax.random.permutation(pair_key, pair_count).astype(jnp.int32)
    first_half = pair_order.reshape(-1, MODES_DEV // 2)
    return jnp.concatenate([first_half, DEGREES - 1 - first_half], axis=1).astype(jnp.int32)


def draw_owned_modes(key, part):
    return ownership(key)


def draw_legendre(key, part):
    mode_list = ownership(key).reshape(-1)
    orders = mode_list.astype(jnp.float32)[:, None]
    row_index = jnp.arange(NT, dtype=jnp.float32)
    colatitude = math.pi * (row_index + 0.5) / NT
    cosine = jnp.cos(colatitude)[None, :]
    sine_row = jnp.sin(colatitude)[None, :]
    log_start = 0.5 * math.log(0.5) + 0.5 * (jax.scipy.special.gammaln(orders + 1.5) - jax.scipy.special.gammaln(jnp.float32(1.5)) - jax.scipy.special.gammaln(orders + 1.0)) + orders * jnp.log(sine_row)
    diagonal_start = jnp.exp(log_start)

    def advance(state_pair, degree_id):
        one_back, two_back = state_pair
        degree = degree_id.astype(jnp.float32)
        denominator = jnp.maximum(degree * degree - orders * orders, 1.0)
        scale_up = jnp.sqrt(jnp.maximum(4.0 * degree * degree - 1.0, 1.0) / denominator)
        lower = degree - 1.0
        scale_back = jnp.sqrt(jnp.maximum(lower * lower - orders * orders, 0.0) / jnp.maximum(4.0 * lower * lower - 1.0, 1.0))
        recurred = scale_up * (cosine * one_back - scale_back * two_back)
        first_step = jnp.sqrt(2.0 * orders + 3.0) * cosine * one_back
        current = jnp.where(degree < orders, 0.0, jnp.where(degree == orders, diagonal_start, jnp.where(degree == orders + 1.0, first_step, recurred)))
        return ((current, one_back), current)
    zeros_start = jnp.zeros((DEGREES, NT), jnp.float32)
    final_pair, stacked = lax.scan(advance, (zeros_start, zeros_start), jnp.arange(DEGREES, dtype=jnp.int32))
    return jnp.transpose(stacked, (1, 2, 0)).astype(jnp.bfloat16)


def draw_radial_inverse(key, part):
    base_key = jax.random.fold_in(key, 5)
    diag_key = jax.random.fold_in(base_key, 1)
    off_key = jax.random.fold_in(base_key, 2)
    degree_scale = jnp.arange(DEGREES, dtype=jnp.float32)[:, None, None] / DEGREES
    off_diag = 0.35 * jax.random.normal(off_key, (DEGREES, SHELLS, SHELLS), jnp.float32) / math.sqrt(SHELLS)
    strength = jax.random.uniform(diag_key, (DEGREES, 1, SHELLS), jnp.float32, 0.5, 1.0) / (1.0 + 2.0 * degree_scale)
    identity = jnp.eye(SHELLS, dtype=jnp.float32)[None, :, :]
    matrix = off_diag * (1.0 - identity) + identity * strength
    return matrix.astype(jnp.bfloat16)


def steps_of(rng, extent, split, smallest, largest):
    gain = 1.0
    for position, blocks in split:
        steps = jax.random.uniform(jax.random.fold_in(jax.random.fold_in(rng, 6), position), (blocks,), jnp.float32, smallest / len(split), largest / len(split))
        gain = gain * jnp.repeat(jnp.exp(steps), extent[position] // blocks).reshape((-1,) + (1,) * (len(extent) - 1 - position))
    return gain


def scatter_about(key, extent, scale, most, shards=(), held_as=jnp.bfloat16):
    entries = scale * jax.random.normal(key, extent, jnp.float32)
    if shards:
        entries = entries * steps_of(key, extent, shards, -0.22, 0.18)
    return jnp.clip(entries, -most, most).astype(held_as)


def setup_inputs(seed: int = 0) -> dict:
    arg_keys = jax.random.split(jax.random.key(seed), 6)
    phase_field = jnp.clip(jax.random.uniform(arg_keys[0], (SHELLS, NT, NP), jnp.float32, -1.0, 1.0) * steps_of(arg_keys[0], (SHELLS, NT, NP), ((1, 8), (2, 4)), -0.4, 0.0), -1.0, 1.0)
    velocity = scatter_about(arg_keys[1], (2, SHELLS, NT, NP), 1.0, 4.0, ((2, 8), (3, 4)))
    owned_modes = draw_owned_modes(jax.random.fold_in(arg_keys[5], 71), 0)
    legendre = draw_legendre(jax.random.fold_in(arg_keys[5], 71), 0)
    radial_inverse = draw_radial_inverse(jax.random.fold_in(arg_keys[5], 71), 0)
    return dict(phase_field=phase_field, velocity=velocity, owned_modes=owned_modes, legendre=legendre, radial_inverse=radial_inverse)


step_time = 2.0e-3
mobility_step = 4.0e-6
highest_precision = lax.Precision.HIGHEST


def shell_radii(shells):
    return 0.75 + 0.25 * (jnp.arange(shells, dtype=jnp.float32) + 0.5) / shells


def colat_weights(count):
    row_index = jnp.arange(count, dtype=jnp.int32)
    waves = jnp.arange(1, count // 2 + 1, dtype=jnp.int32)
    turns = ((2 * row_index[:, None] + 1) * waves[None, :]) % (2 * count)
    cosines = jnp.cos(turns.astype(jnp.float32) * (math.pi / count))
    wave_float = waves.astype(jnp.float32)
    coefs = 1.0 / (4.0 * wave_float * wave_float - 1.0)
    return (2.0 / count) * (1.0 - 2.0 * jnp.dot(cosines, coefs, precision=highest_precision))


def reference(phase_field, velocity, owned_modes, legendre, radial_inverse):
    shells, theta_count, phi_count = phase_field.shape
    mode_list = owned_modes.reshape(-1).astype(jnp.int32)
    mode_count = mode_list.shape[0]
    degree_count = legendre.shape[2]
    legendre_full = legendre.astype(jnp.float32)
    shell_radius = shell_radii(shells)
    east_cell = jnp.roll(phase_field, -1, axis=2)
    west_cell = jnp.roll(phase_field, 1, axis=2)
    padded = jnp.pad(phase_field, ((0, 0), (1, 1), (0, 0)))
    south_cell = padded[:, 2:, :]
    north_cell = padded[:, :-2, :]
    d_phi = (east_cell - west_cell) * (phi_count / (4.0 * math.pi))
    d_theta = (south_cell - north_cell) * (theta_count / (2.0 * math.pi))
    spin_rate = velocity[0].astype(jnp.float32)
    sweep_speed = velocity[1].astype(jnp.float32)
    advected = phase_field - step_time * (spin_rate * d_phi + sweep_speed / shell_radius[:, None, None] * d_theta)
    potential = phase_field * phase_field * phase_field - phase_field
    fields = jnp.stack([advected, potential])
    spectrum = jnp.fft.rfft(fields, axis=-1) / phi_count
    picked = spectrum[..., mode_list]
    real_imag = jnp.stack([jnp.real(picked), jnp.imag(picked)]).astype(jnp.float32)
    arranged = jnp.transpose(real_imag, (4, 3, 0, 1, 2)).reshape(mode_count, theta_count, 4 * shells)
    weights = colat_weights(theta_count)
    weighted = arranged * weights[None, :, None]
    coeffs = jnp.einsum("ktx,ktl->klx", weighted.astype(jnp.float32), legendre_full, precision=highest_precision)
    coeffs = coeffs.reshape(mode_count, degree_count, 2, 2, shells)
    degrees = jnp.arange(degree_count, dtype=jnp.float32)
    factor = mobility_step * (degrees * (degrees + 1.0))[:, None] / (shell_radius * shell_radius)[None, :]
    right_side = coeffs[:, :, :, 0, :] - factor[None, :, None, :] * coeffs[:, :, :, 1, :]
    solved = jnp.einsum("lrs,klqs->klqr", radial_inverse.astype(jnp.float32), right_side, precision=highest_precision)
    synthesis = jnp.einsum("ktl,klx->ktx", legendre_full, solved.reshape(mode_count, degree_count, 2 * shells), precision=highest_precision)
    synthesis = synthesis.reshape(mode_count, theta_count, 2, shells)
    natural = jnp.argsort(mode_list)
    ordered = synthesis[natural]
    real_part = jnp.transpose(ordered[:, :, 0, :], (2, 1, 0))
    imag_part = jnp.transpose(ordered[:, :, 1, :], (2, 1, 0))
    complex_modes = lax.complex(real_part, imag_part)
    padded_modes = jnp.pad(complex_modes, ((0, 0), (0, 0), (0, phi_count // 2 + 1 - mode_count)))
    new_phase = phi_count * jnp.fft.irfft(padded_modes, n=phi_count, axis=-1)
    return new_phase.astype(jnp.float32)
```

```python
import functools
import math

import jax
import jax.numpy as jnp
from jax import lax
from jax.experimental import pallas as pl
from jax.experimental.pallas import tpu as pltpu
from jax.sharding import PartitionSpec as P

step_time = 0.002
mobility_step = 4e-06
highest_precision = lax.Precision.HIGHEST
vmem_limit = 48 * 1024 * 1024
chunk_count = 4


def shell_radii(shells):
    return 0.75 + 0.25 * (jnp.arange(shells, dtype=jnp.float32) + 0.5) / shells


def colat_weights(count):
    row_index = jnp.arange(count, dtype=jnp.int32)
    waves = jnp.arange(1, count // 2 + 1, dtype=jnp.int32)
    turns = (2 * row_index[:, None] + 1) * waves[None, :] % (2 * count)
    cosines = jnp.cos(turns.astype(jnp.float32) * (math.pi / count))
    wave_float = waves.astype(jnp.float32)
    coefs = 1.0 / (4.0 * wave_float * wave_float - 1.0)
    return 2.0 / count * (1.0 - 2.0 * jnp.dot(cosines, coefs, precision=highest_precision))


def split_bf16(value):
    high = value.astype(jnp.bfloat16)
    low = (value - high.astype(jnp.float32)).astype(jnp.bfloat16)
    return high, low


def split_rounded(value):
    high = lax.reduce_precision(value, exponent_bits=8, mantissa_bits=7)
    return high.astype(jnp.bfloat16), (value - high).astype(jnp.bfloat16)


def dot_nt(a, b):
    return lax.dot_general(a, b, (((1,), (1,)), ((), ())), preferred_element_type=jnp.float32)


def dot_nn(a, b):
    return jnp.dot(a, b, preferred_element_type=jnp.float32)


def grid_kernel(shells, phi_count, theta_count, off_ref, c_ref, v_ref, rows_ref, cols_ref, o_ref):
    c = c_ref[0]
    theta_local, phi_local = c.shape
    lane = lax.broadcasted_iota(jnp.int32, c.shape, 1)
    row = lax.broadcasted_iota(jnp.int32, c.shape, 0)
    east = jnp.where(lane == phi_local - 1, cols_ref[0, :, 1:2], pltpu.roll(c, phi_local - 1, 1))
    west = jnp.where(lane == 0, cols_ref[0, :, 0:1], pltpu.roll(c, 1, 1))
    south = jnp.where(row == theta_local - 1, rows_ref[0, 1:2, :], pltpu.roll(c, theta_local - 1, 0))
    north = jnp.where(row == 0, rows_ref[0, 0:1, :], pltpu.roll(c, 1, 0))
    d_phi = (east - west) * (phi_count / (4.0 * math.pi))
    d_theta = (south - north) * (theta_count / (2.0 * math.pi))
    shell = jnp.full((1, 1), off_ref[0] + pl.program_id(0), jnp.int32).astype(jnp.float32)
    inverse_radius = 1.0 / (0.75 + 0.25 * (shell + 0.5) / shells)
    spin_rate = v_ref[0, 0].astype(jnp.float32)
    sweep_speed = v_ref[1, 0].astype(jnp.float32)
    o_ref[0, 0] = c - step_time * (spin_rate * d_phi + sweep_speed * inverse_radius * d_theta)
    o_ref[1, 0] = c * c * c - c


def grid_fields(phase_field, velocity, rows, cols, offset, count, phi_count, theta_count):
    shells, theta_local, phi_local = phase_field.shape
    return pl.pallas_call(
        functools.partial(grid_kernel, shells, phi_count, theta_count),
        grid_spec=pltpu.PrefetchScalarGridSpec(
            num_scalar_prefetch=1,
            grid=(count,),
            in_specs=[
                pl.BlockSpec((1, theta_local, phi_local), lambda i, off: (off[0] + i, 0, 0)),
                pl.BlockSpec((2, 1, theta_local, phi_local), lambda i, off: (0, off[0] + i, 0, 0)),
                pl.BlockSpec((1, 2, phi_local), lambda i, off: (off[0] + i, 0, 0)),
                pl.BlockSpec((1, theta_local, 2), lambda i, off: (off[0] + i, 0, 0)),
            ],
            out_specs=pl.BlockSpec((2, 1, theta_local, phi_local), lambda i, off: (0, i, 0, 0)),
        ),
        out_shape=jax.ShapeDtypeStruct((2, count, theta_local, phi_local), jnp.float32),
        compiler_params=pltpu.CompilerParams(vmem_limit_bytes=vmem_limit),
        cost_estimate=pl.CostEstimate(
            flops=20 * count * theta_local * phi_local,
            bytes_accessed=16 * count * theta_local * phi_local,
            transcendentals=0,
        ),
    )(offset.reshape(1), phase_field, velocity, rows, cols)


def forward_kernel(own_ref, other_ref, high_ref, low_ref, o_ref):
    _, block, theta_local, phi_local = own_ref.shape
    own = own_ref[0].reshape(block * theta_local, phi_local)
    other = other_ref[0].reshape(block * theta_local, phi_local)
    high, low = split_bf16(jnp.concatenate([own, other], axis=1))
    sums = dot_nt(high_ref[...], high) + dot_nt(high_ref[...], low) + dot_nt(low_ref[...], high)
    classes, cols, _, _, pairs, _ = o_ref.shape
    for j in range(block):
        part = sums[:, j * theta_local : (j + 1) * theta_local]
        o_ref[:, :, 0, j] = part.reshape(classes, cols, pairs, theta_local)


def forward_sums(own, other, high, low, cols, pairs):
    fields, count, theta_local, phi_local = own.shape
    rows = high.shape[0]
    classes = rows // (cols * pairs)
    block = 4
    field_spec = pl.BlockSpec((1, block, theta_local, phi_local), lambda f, i: (f, i, 0, 0))
    table_spec = pl.BlockSpec((rows, 2 * phi_local), lambda f, i: (0, 0))
    return pl.pallas_call(
        forward_kernel,
        grid=(fields, count // block),
        in_specs=[field_spec, field_spec, table_spec, table_spec],
        out_specs=pl.BlockSpec(
            (classes, cols, 1, block, pairs, theta_local), lambda f, i: (0, 0, f, i, 0, 0)
        ),
        out_shape=jax.ShapeDtypeStruct(
            (classes, cols, fields, count, pairs, theta_local), jnp.float32
        ),
        compiler_params=pltpu.CompilerParams(vmem_limit_bytes=vmem_limit),
        cost_estimate=pl.CostEstimate(
            flops=12 * rows * fields * count * theta_local * phi_local,
            bytes_accessed=8 * own.size + 4 * rows * fields * count * theta_local,
            transcendentals=0,
        ),
    )(own, other, high, low)


def inverse_kernel(here_ref, there_ref, high_ref, low_ref, keep_ref, send_ref):
    block, theta_local, phi_local = keep_ref.shape
    parts = []
    for j in range(block):
        here = here_ref[:, :, j].reshape(-1, theta_local)
        there = there_ref[:, :, j].reshape(-1, theta_local)
        parts.append(jnp.concatenate([here, there], axis=0).T)
    high, low = split_bf16(jnp.concatenate(parts, axis=0))
    values = dot_nn(high, high_ref[...]) + dot_nn(high, low_ref[...]) + dot_nn(low, high_ref[...])
    keep_ref[...] = values[:, :phi_local].reshape(block, theta_local, phi_local)
    send_ref[...] = values[:, phi_local:].reshape(block, theta_local, phi_local)


def inverse_sums(here, there, high, low):
    classes, cols, count, pairs, theta_local = here.shape
    rows, phi_two = high.shape
    block = 4
    half_spec = pl.BlockSpec(
        (classes, cols, block, pairs, theta_local), lambda i: (0, 0, i, 0, 0)
    )
    table_spec = pl.BlockSpec((rows, phi_two), lambda i: (0, 0))
    out_spec = pl.BlockSpec((block, theta_local, phi_two // 2), lambda i: (i, 0, 0))
    out_type = jax.ShapeDtypeStruct((count, theta_local, phi_two // 2), jnp.float32)
    return pl.pallas_call(
        inverse_kernel,
        grid=(count // block,),
        in_specs=[half_spec, half_spec, table_spec, table_spec],
        out_specs=[out_spec, out_spec],
        out_shape=[out_type, out_type],
        compiler_params=pltpu.CompilerParams(vmem_limit_bytes=vmem_limit),
        cost_estimate=pl.CostEstimate(
            flops=6 * rows * count * theta_local * phi_two,
            bytes_accessed=8 * here.size + 4 * count * theta_local * phi_two,
            transcendentals=0,
        ),
    )(here, there, high, low)


def swap_az(value, bit):
    count = lax.axis_size("az")
    return lax.ppermute(value, "az", [(i, i ^ (1 << bit)) for i in range(count)])


def body(phase_field, velocity, owned_modes, legendre, radial_inverse):
    shells, theta_local, phi_local = phase_field.shape
    az_count = lax.axis_size("az")
    col_count = lax.axis_size("col")
    az_here = lax.axis_index("az")
    col_here = lax.axis_index("col")
    bits = az_count.bit_length() - 1
    phi_count = phi_local * az_count
    theta_count = theta_local * col_count
    mode_dev, _, degree_count = legendre.shape
    pairs = 2 * mode_dev
    shell_radius = shell_radii(shells)

    east_going = [(i, (i + 1) % az_count) for i in range(az_count)]
    west_going = [(j, i) for i, j in east_going]
    south_going = [(i, i + 1) for i in range(col_count - 1)]
    north_going = [(j, i) for i, j in south_going]
    west_col = lax.ppermute(phase_field[:, :, phi_local - 1], "az", east_going)
    east_col = lax.ppermute(phase_field[:, :, 0], "az", west_going)
    north_row = lax.ppermute(phase_field[:, theta_local - 1, :], "col", south_going)
    south_row = lax.ppermute(phase_field[:, 0, :], "col", north_going)
    north_row = jnp.where(col_here == 0, 0.0, north_row)
    south_row = jnp.where(col_here == col_count - 1, 0.0, south_row)
    rows = jnp.stack([north_row, south_row], axis=1)
    cols = jnp.stack([west_col, east_col], axis=2)

    mode_table = owned_modes.reshape(az_count, col_count * mode_dev)
    local_phi = jnp.arange(phi_local, dtype=jnp.int32)

    def tables(pair_bit):
        rest = [k for k in range(bits) if k != pair_bit]
        order = [0, 1 << pair_bit]
        for k in reversed(rest):
            order = order + [d | (1 << k) for d in order]
        modes = jnp.concatenate(
            [lax.dynamic_index_in_dim(mode_table, az_here ^ d, 0, keepdims=False) for d in order]
        )
        phi = jnp.concatenate(
            [az_here * phi_local + local_phi, (az_here ^ (1 << pair_bit)) * phi_local + local_phi]
        )
        turns = modes[:, None, None] * phi[None, None, :] % phi_count
        quarter = jnp.arange(2, dtype=jnp.int32)[None, :, None] * (phi_count // 4)
        turns = (turns + quarter) % phi_count
        wave = jnp.cos(turns.astype(jnp.float32) * (2.0 * math.pi / phi_count))
        wave = wave.reshape(2 * modes.shape[0], 2 * phi_local)
        high, low = split_rounded(wave)
        gain = jnp.where(modes == 0, 1.0, 2.0).astype(jnp.bfloat16)
        gain = jnp.repeat(gain, 2)[:, None]
        scale = jnp.bfloat16(1.0 / phi_count)
        return rest, (high * scale, low * scale), (high * gain, low * gain)

    pair_bits = [j % bits for j in range(chunk_count)]
    plans = {b: tables(b) for b in sorted(set(pair_bits))}

    chunk = shells // chunk_count
    half = chunk // 2
    weights = colat_weights(theta_count)
    degrees = jnp.arange(degree_count, dtype=jnp.float32)
    degree_factor = degrees * (degrees + 1.0)

    def to_cols(value):
        return lax.all_to_all(value, "col", split_axis=0, concat_axis=0, tiled=True)

    right_sides = []
    for j, b in enumerate(pair_bits):
        rest, (high, low), _ = plans[b]
        mine = (az_here >> b) & 1
        make = functools.partial(
            grid_fields, phase_field, velocity, rows, cols,
            count=half, phi_count=phi_count, theta_count=theta_count,
        )
        other = swap_az(make(offset=j * chunk + (1 - mine) * half), b)
        own = make(offset=j * chunk + mine * half)
        cut = high.shape[0] // 2
        sums = swap_az(forward_sums(own, other, high[cut:], low[cut:], col_count, pairs), rest[0])
        sums = sums + forward_sums(own, other, high[:cut], low[:cut], col_count, pairs)
        for k in rest[1:]:
            middle = sums.shape[0] // 2
            sums = sums[:middle] + swap_az(sums[middle:], k)
        mine_half = to_cols(sums[0])
        other_half = to_cols(swap_az(sums[1], b))
        first = jnp.where(mine == 0, mine_half, other_half)
        second = jnp.where(mine == 0, other_half, mine_half)
        both = jnp.concatenate([first, second], axis=2)
        both = both.reshape(col_count, 2, chunk, mode_dev, 2, theta_local)
        both = jnp.transpose(both, (3, 1, 4, 2, 0, 5))
        both = both.reshape(mode_dev, 4 * chunk, theta_count) * weights
        lhs = jnp.concatenate(split_rounded(both), axis=1)
        coeffs = jnp.einsum("qxt,qtl->qxl", lhs, legendre, preferred_element_type=jnp.float32)
        coeffs = coeffs[:, : 4 * chunk] + coeffs[:, 4 * chunk :]
        coeffs = coeffs.reshape(mode_dev, 2, 2, chunk, degree_count)
        radius = shell_radius[j * chunk : (j + 1) * chunk]
        factor = mobility_step * degree_factor[None, :] / (radius * radius)[:, None]
        right_sides.append(coeffs[:, 0] - factor * coeffs[:, 1])

    right_side = jnp.concatenate(right_sides, axis=2)
    right_side = jnp.transpose(right_side, (3, 2, 0, 1)).reshape(degree_count, shells, pairs)
    rhs = jnp.concatenate(split_rounded(right_side), axis=2)
    solved = jnp.einsum("lrs,lsn->lrn", radial_inverse, rhs, preferred_element_type=jnp.float32)
    solved = solved[:, :, :pairs] + solved[:, :, pairs:]
    solved = jnp.transpose(solved.reshape(degree_count, shells, mode_dev, 2), (2, 1, 3, 0))

    pieces = []
    for j, b in enumerate(pair_bits):
        rest, _, (high, low) = plans[b]
        mine = (az_here >> b) & 1
        part = solved[:, j * chunk : (j + 1) * chunk].reshape(mode_dev, 2 * chunk, degree_count)
        lhs = jnp.concatenate(split_rounded(part), axis=1)
        grid_modes = jnp.einsum("qxl,qtl->qxt", lhs, legendre, preferred_element_type=jnp.float32)
        grid_modes = grid_modes[:, : 2 * chunk] + grid_modes[:, 2 * chunk :]
        grid_modes = grid_modes.reshape(mode_dev, 2, half, 2, col_count, theta_local)
        grid_modes = jnp.transpose(grid_modes, (1, 4, 2, 0, 3, 5))
        grid_modes = grid_modes.reshape(2, col_count, half, pairs, theta_local)
        keep_half = to_cols(jnp.where(mine == 0, grid_modes[0], grid_modes[1]))
        send_half = swap_az(to_cols(jnp.where(mine == 0, grid_modes[1], grid_modes[0])), b)
        here = jnp.stack([keep_half, send_half])
        there = None
        for k in reversed(rest):
            if there is not None:
                here = jnp.concatenate([here, there])
            there = swap_az(here, k)
        keep, send = inverse_sums(here, there, high, low)
        arrived = swap_az(send, b)
        pieces.append(jnp.where(mine == 0, keep, arrived))
        pieces.append(jnp.where(mine == 0, arrived, keep))
    return jnp.concatenate(pieces, axis=0)


def solution(mesh):
    in_specs = (
        P(None, "col", "az"),
        P(None, None, "col", "az"),
        P(),
        P(("az", "col"), None, None),
        P(),
    )
    out_specs = P(None, "col", "az")
    return jax.shard_map(body, mesh=mesh, in_specs=in_specs, out_specs=out_specs, check_vma=False)
```
